32 devices in a mesh: tp: 4 (over x, core), cp: 8 (over z, y).
Axes of the slice: x: 2, y: 2, z: 4, core: 2. Of those that a mesh axis runs over, the one named last changes fastest.
Arguments:
- grad_out: bfloat16 [4, 1024, 4096], P('tp', 'cp'), may hold values from -6 to 6
- expert_ids: int32 [4, 1024, 8], P('tp', 'cp'), may hold values from 0 to 31, all different within a row; in each aligned block of 128 rows (0 to 127, 128 to 255, ..., all dimensions but the last counted through in order) at most 40 rows name the same one
- route_prob: bfloat16 [4, 1024, 8], P('tp', 'cp'), may hold values from 0.049804688 to 0.5
- attn_out: bfloat16 [4096, 4096], P('cp', 'tp'), may hold values from -0.09375 to 0.09375
- w_down: bfloat16 [32, 768, 4096], P(('tp', 'cp')), may hold values from -0.09375 to 0.09375
- hidden_saved: bfloat16 [32, 1280, 768], P(('tp', 'cp')), may hold values from -0.21875 to 0.21875
Outputs:
- grad_prob: float32 [4, 1024, 8], P('tp', 'cp')
- grad_hidden: bfloat16 [32, 1280, 768], P(('tp', 'cp'))
- grad_down: bfloat16 [32, 768, 4096], P(('tp', 'cp'))
- grad_oproj: bfloat16 [4096, 4096], P('cp', 'tp')
The draws below stay inside these ranges and needn't reach their ends.
Inputs may be any that keep to these rules, and one draw needn't show every extreme that they name: `expert_ids`: within each device's block of 128 tokens, no expert is named by more than 40 routes, and in every draw some expert is named by exactly 40; every expert is named somewhere.
All inputs are finite; a program needn't handle non-finite values.
Results may differ from the reference program's by a relative error of at most 0.0049.
Values may be sent and summed in bfloat16 or wider, within the bound.
A program may use at most 192 MiB of HBM per device.

```python
import math
import jax
import jax.numpy as jnp
import numpy as np
from jax import lax

D = 4096
HID = 768
TOP = 8
TOK_DEV = 128
EXPERTS = 32
CAP = 40
SLOTS = 1280
HQD = 4096
CTX = 1024
TOKENS = 4096
N_TP = 4
N_CP = 8


def levels(stream_key, dims, split, low, high):
    level = 1.0
    for dim, blocks in split:
        draws = jax.random.uniform(jax.random.fold_in(jax.random.fold_in(stream_key, 6), dim), (blocks,), jnp.float32, low / len(split), high / len(split))
        level = level * jnp.repeat(jnp.exp(draws), dims[dim] // blocks).reshape((-1,) + (1,) * (len(dims) - 1 - dim))
    return level


def shared_out(key, own, number, rows, number_of, top, bound, lean):
    ranking = jax.random.permutation(key, number_of)
    crowded, usual = shares(number_of, rows * top, bound, lean, True), shares(number_of, rows * top, bound, lean, False)
    places = jnp.arange(number_of)

    def named(sizes, rotation):
        used = int((sizes > 0).sum())
        fixed = max(1, used // 4)
        moved = fixed + (places - fixed + rotation * (used - fixed)) % max(1, number_of - fixed)
        return jnp.zeros((number_of,), jnp.int32).at[ranking[jnp.where(places < fixed, places, moved)]].set(jnp.asarray(sizes, jnp.int32))

    sizes = jnp.where(number % 4 == 0, named(crowded, number // 4), named(usual, number - number // 4 - 1))
    mixed = jax.random.permutation(jax.random.fold_in(own, 3), number_of)
    giver, sink = mixed[0:number_of // 2 * 2:2], mixed[1:number_of // 2 * 2:2]
    room = jnp.minimum(sizes[giver] - 1, bound - sizes[sink]) // 2
    room = jnp.where((giver == ranking[0]) | (sink == ranking[0]) | (sizes[sink] == 0), 0, jnp.maximum(room, 0))
    moved = jax.random.randint(jax.random.fold_in(own, 4), (number_of // 2,), 0, 1 << 20) % (room + 1)
    sizes = sizes.at[giver].add(-moved).at[sink].add(moved)
    labels = jnp.searchsorted(jnp.cumsum(sizes), jnp.arange(rows * top), side="right").astype(jnp.int32)
    table = labels.reshape(top, rows).T
    table = table[jax.random.permutation(jax.random.fold_in(own, 1), rows)]
    rotation = jax.random.randint(jax.random.fold_in(own, 2), (rows, 1), 0, top)
    return jnp.take_along_axis(table, (jnp.arange(top)[None, :] + rotation) % top, axis=1)


def shares(count, total, bound, slope, full):
    loads = [(1 << 20) // math.isqrt(rank ** slope) + 1 for rank in range(1, count + 1)]
    largest = bound if full else min(bound, max(-(-total // count), total * loads[0] // sum(loads)))
    least = 1 if total - largest >= count - 1 else 0
    given, surplus = [largest] + [least] * (count - 1), total - largest - least * (count - 1)
    while surplus > 0:
        candidates = [i for i in range(1, count) if given[i] < largest] or [i for i in range(1, count) if given[i] < bound]
        whole, left = sum([loads[i] for i in candidates]), surplus
        for i in candidates:
            more = min(bound - given[i], max(1, left * loads[i] // whole), surplus)
            given[i] = given[i] + more
            surplus = surplus - more
    return np.array(given)


def bell_draw(own_key, dims, width, most, split=(), kind=jnp.bfloat16):
    entries = jax.random.normal(own_key, dims, jnp.float32) * width
    if len(split) > 0:
        entries = levels(own_key, dims, split, -0.22, 0.18) * entries
    return jnp.clip(entries, min=-most, max=most).astype(kind)


def setup_inputs(seed: int = 0) -> dict:
    seeds = jax.random.split(jax.random.key(seed), 7)
    grad_out = bell_draw(seeds[0], (N_TP, CTX, D), 1.0, 6.0, ((0, 4), (1, 8)))
    expert_ids_keys = jax.random.split(jax.random.fold_in(seeds[1], 1), N_TP * CTX // TOK_DEV)
    expert_ids_turns = jax.random.permutation(jax.random.fold_in(seeds[1], 3), N_TP * CTX // TOK_DEV)
    expert_ids = jax.vmap(lambda own, number: shared_out(jax.random.fold_in(seeds[1], 2), own, number, TOK_DEV, N_TP * N_CP, TOP, CAP, 2))(expert_ids_keys, expert_ids_turns).reshape((N_TP, CTX, TOP))
    route_prob = jnp.clip(0.049804688 + 0.4501953 * jax.random.uniform(seeds[2], (N_TP, CTX, TOP), jnp.float32) ** levels(seeds[2], (N_TP, CTX, TOP), ((0, 4), (1, 8)), -0.2, 0.2), 0.049804688, 0.5).astype(jnp.bfloat16)
    attn_out = bell_draw(seeds[3], (TOKENS, HQD), TOKENS ** -0.5, 0.09375, ((0, 8), (1, 4)))
    w_down = bell_draw(seeds[4], (EXPERTS, HID, D), D ** -0.5, 0.09375, ((0, 32),))
    hidden_saved = bell_draw(seeds[5], (EXPERTS, SLOTS, HID), HID ** -0.5, 0.21875, ((0, 32),))
    return {"grad_out": grad_out, "expert_ids": expert_ids, "route_prob": route_prob, "attn_out": attn_out, "w_down": w_down, "hidden_saved": hidden_saved}


def reference(grad_out, expert_ids, route_prob, attn_out, w_down, hidden_saved):
    n_experts = N_TP * N_CP
    per_block = TOK_DEV * TOP
    block_ids = expert_ids.reshape(n_experts, per_block)
    onehot = (block_ids[:, :, None] == jnp.arange(n_experts, dtype=jnp.int32)[None, None, :]).astype(jnp.int32)
    position = jnp.sum((jnp.cumsum(onehot, axis=1) - 1) * onehot, axis=2)
    slot_of = (jnp.arange(n_experts, dtype=jnp.int32)[:, None] * CAP + position).reshape(-1).astype(jnp.int32)
    flat_ids = block_ids.reshape(-1)
    token_of = (jnp.arange(n_experts * per_block, dtype=jnp.int32) // TOP).astype(jnp.int32)
    rows_all = grad_out.reshape(-1, D)
    probs_all = route_prob.reshape(-1).astype(jnp.float32)

    def per_expert(expert):
        target = jnp.where(flat_ids == expert, slot_of, SLOTS).astype(jnp.int32)
        source = jnp.zeros((SLOTS + 1,), jnp.int32).at[target].set(token_of)[:SLOTS]
        live = jnp.zeros((SLOTS + 1,), jnp.float32).at[target].set(1.0)[:SLOTS]
        weight = jnp.zeros((SLOTS + 1,), jnp.float32).at[target].set(probs_all)[:SLOTS]
        routed = jnp.where(live[:, None] > 0.5, rows_all[source], jnp.zeros((), jnp.bfloat16)).astype(jnp.bfloat16)
        proj = jnp.dot(routed, w_down[expert].T, preferred_element_type=jnp.float32)
        grad_hid = (weight[:, None] * proj).astype(jnp.bfloat16)
        prob_part = jnp.sum(proj * hidden_saved[expert].astype(jnp.float32), axis=1)
        weighted = (weight[:, None] * routed.astype(jnp.float32)).astype(jnp.bfloat16)
        grad_w = jnp.dot(hidden_saved[expert].T, weighted, preferred_element_type=jnp.float32).astype(jnp.bfloat16)
        return grad_hid, prob_part, grad_w

    grad_hidden, prob_parts, grad_down = lax.map(per_expert, jnp.arange(n_experts, dtype=jnp.int32))
    lookup = (flat_ids * SLOTS + slot_of).astype(jnp.int32)
    grad_prob = prob_parts.reshape(-1)[lookup].reshape(N_TP, CTX, TOP)
    ordered = grad_out.reshape(N_TP, N_CP, TOK_DEV, D).transpose(1, 0, 2, 3).reshape(TOKENS, D)
    grad_oproj = jnp.dot(ordered.T, attn_out, preferred_element_type=jnp.float32).astype(jnp.bfloat16)
    return grad_prob, grad_hidden, grad_down, grad_oproj
```

```python
import functools

import jax
import jax.numpy as jnp
from jax import lax
from jax.experimental import pallas as pl
from jax.experimental.pallas import tpu as pltpu
from jax.sharding import PartitionSpec as P

MESH = pl.DeviceIdType.MESH


def exchange_local(grad_out, expert_ids, route_prob, attn_out, w_down, hidden_saved):
    tp_count = lax.axis_size("tp")
    cp_count = lax.axis_size("cp")
    n_experts = tp_count * cp_count
    slot_count = hidden_saved.shape[1]
    capacity = slot_count // n_experts
    local_rows = grad_out[0]
    token_count = local_rows.shape[0]
    width = local_rows.shape[1]
    top_count = expert_ids.shape[2]
    route_ids = expert_ids[0].reshape(-1)
    onehot = (route_ids[:, None] == jnp.arange(n_experts, dtype=jnp.int32)[None, :]).astype(
        jnp.int32
    )
    position = jnp.sum((jnp.cumsum(onehot, axis=0) - 1) * onehot, axis=1)
    target = route_ids * capacity + position
    token_of = jnp.arange(token_count * top_count, dtype=jnp.int32) // top_count
    send_rows = (
        jnp.zeros((n_experts * capacity, width), jnp.bfloat16).at[target].set(local_rows[token_of])
    )
    send_prob = (
        jnp.zeros((n_experts * capacity,), jnp.bfloat16).at[target].set(route_prob[0].reshape(-1))
    )

    def swap(value):
        return lax.all_to_all(value, ("tp", "cp"), split_axis=0, concat_axis=0, tiled=True)

    routed = swap(send_rows.reshape(n_experts, capacity, width)).reshape(slot_count, width)
    got_prob = swap(send_prob.reshape(n_experts, capacity))
    weight = got_prob.reshape(slot_count).astype(jnp.float32)[:, None]
    saved = hidden_saved[0]
    proj = lax.dot_general(
        routed, w_down[0], (((1,), (1,)), ((), ())), preferred_element_type=jnp.float32
    )
    grad_hid = (weight * proj).astype(jnp.bfloat16)
    prob_part = jnp.sum(proj * saved.astype(jnp.float32), axis=1)
    weighted = (weight * routed.astype(jnp.float32)).astype(jnp.bfloat16)
    grad_w = lax.dot_general(
        saved, weighted, (((0,), (0,)), ((), ())), preferred_element_type=jnp.float32
    ).astype(jnp.bfloat16)
    returned = swap(prob_part.reshape(n_experts, capacity))
    grad_prob = returned.reshape(-1)[target].reshape(1, token_count, top_count)
    gathered = lax.all_gather(grad_out, "tp", axis=0, tiled=True).reshape(-1, width)
    grad_oproj = lax.psum_scatter(
        lax.dot_general(
            gathered, attn_out, (((0,), (0,)), ((), ())), preferred_element_type=jnp.float32
        ),
        "cp",
        scatter_dimension=0,
        tiled=True,
    ).astype(jnp.bfloat16)
    return (grad_prob, grad_hid[None], grad_w[None], grad_oproj)


def gather_kernel(n_tp, n_cp, g_ref, a_ref, gall, aall, gz_l, gz_r, gy_s, gx_s, gs_s, az_l, az_r, ay_s, g_recv, a_recv, own_sem):
    t = lax.axis_index("tp")
    c = lax.axis_index("cp")
    core = t % 2
    x = t // 2
    y = c % 2
    z = c // 2
    nz = n_cp // 2
    sib = t + 1 - 2 * core
    xt = (1 - x) * 2 + core
    yc = z * 2 + 1 - y
    has_l = z > 0
    has_r = z < nz - 1

    barrier = pltpu.get_barrier_semaphore()

    def greet(tt, cc):
        pl.semaphore_signal(barrier, inc=1, device_id=(tt, cc), device_id_type=MESH)

    greet(sib, c)
    greet(xt, c)
    greet(t, yc)

    @pl.when(has_l)
    def _():
        greet(t, c - 2)

    @pl.when(has_r)
    def _():
        greet(t, c + 2)

    pl.semaphore_wait(barrier, 3 + has_l.astype(jnp.int32) + has_r.astype(jnp.int32))

    def pick(values):
        got = values[0]
        for k in range(1, nz):
            got = jnp.where(z == k, values[k], got)
        return got

    lists = []
    for p in range(nz):
        lists.append(sorted(range(nz), key=lambda q, p=p: (abs(q - p), q)))
    order = [z] + [pick([lists[p][i] for p in range(nz)]) for i in range(1, nz)]

    def gblock(tt, zz, yy):
        return tt * n_cp + zz * 2 + yy

    def gcopy(b, src, send, dev):
        return pltpu.make_async_remote_copy(
            src_ref=src, dst_ref=gall.at[b], send_sem=send, recv_sem=g_recv.at[b], device_id=dev, device_id_type=MESH
        )

    def acopy(k, src, send, dev):
        return pltpu.make_async_remote_copy(
            src_ref=src, dst_ref=aall.at[k], send_sem=send, recv_sem=a_recv.at[k], device_id=dev, device_id_type=MESH
        )

    mine = gblock(t, z, y)
    own_g = pltpu.make_async_copy(g_ref, gall.at[mine], own_sem.at[0])
    own_a = pltpu.make_async_copy(a_ref, aall.at[c], own_sem.at[1])
    own_g.start()
    own_a.start()
    sends = []

    def line(copier, left, right, i, idx, src):
        def go(sem, dc, cond):
            op = copier(idx, src, sem.at[i], (t, c + dc))

            @pl.when(cond)
            def _():
                op.start()

            sends.append((op, cond))

        zi = order[i]
        if i == 0:
            go(left, -2, has_l)
            go(right, 2, has_r)
        else:
            go(left, -2, jnp.logical_and(zi > z, has_l))
            go(right, 2, jnp.logical_and(zi < z, has_r))

    def plain(op):
        op.start()
        sends.append((op, None))

    nx = [0]
    ns = [0]

    def to_x(b, src):
        plain(gcopy(b, src, gx_s.at[nx[0]], (xt, c)))
        nx[0] += 1

    def to_sib(b, src):
        plain(gcopy(b, src, gs_s.at[ns[0]], (sib, c)))
        ns[0] += 1

    def z_event(i):
        b = gblock(t, order[i], y)
        if i == 0:
            src = g_ref
        else:
            src = gall.at[b]
            gcopy(b, src, gy_s.at[0], (t, c)).wait_recv()
        line(gcopy, gz_l, gz_r, i, b, src)
        plain(gcopy(b, src, gy_s.at[i], (t, yc)))
        to_x(b, src)
        to_sib(b, src)

    def y_event(i):
        b = gblock(t, order[i], 1 - y)
        gcopy(b, gall.at[b], gy_s.at[0], (t, c)).wait_recv()
        to_x(b, gall.at[b])
        to_sib(b, gall.at[b])

    xseq = [(0, y)]
    for i in range(1, nz):
        xseq += [(i, y), (i - 1, 1 - y)]
    xseq.append((nz - 1, 1 - y))

    def x_event(k):
        i, yy = xseq[k]
        b = gblock(xt, order[i], yy)
        gcopy(b, gall.at[b], gy_s.at[0], (t, c)).wait_recv()
        to_sib(b, gall.at[b])

    def az_event(i):
        k = order[i] * 2 + y
        if i == 0:
            src = a_ref
        else:
            src = aall.at[k]
            acopy(k, src, ay_s.at[0], (t, c)).wait_recv()
        line(acopy, az_l, az_r, i, k, src)
        plain(acopy(k, src, ay_s.at[i], (t, yc)))

    z_event(0)
    for r in range(1, nz):
        z_event(r)
        y_event(r - 1)
        x_event(r - 1)
    az_event(0)
    y_event(nz - 1)
    x_event(nz - 1)
    for r in range(nz, 2 * nz):
        if r - nz + 1 < nz:
            az_event(r - nz + 1)
        if r >= nz + 0 and r < 2 * nz:
            if r > nz - 1 and r != nz - 1 and r < 2 * nz:
                x_event(r)
    for i in range(nz):
        k = order[i] * 2 + 1 - y
        acopy(k, aall.at[k], ay_s.at[0], (t, c)).wait_recv()

    for zz in range(nz):
        for yy in range(2):
            for xx in range(2):
                b = gblock(xx * 2 + 1 - core, zz, yy)
                gcopy(b, gall.at[b], gy_s.at[0], (t, c)).wait_recv()
    for op, cond in sends:
        if cond is None:
            op.wait_send()
        else:

            @pl.when(cond)
            def _(op=op):
                op.wait_send()

    own_g.wait()
    own_a.wait()


def gather_all(n_tp, n_cp, rows, attn):
    nz = n_cp // 2
    dma = pltpu.SemaphoreType.DMA
    n_dev = n_tp * n_cp
    return pl.pallas_call(
        functools.partial(gather_kernel, n_tp, n_cp),
        out_shape=(
            jax.ShapeDtypeStruct((n_dev,) + rows.shape, rows.dtype),
            jax.ShapeDtypeStruct((n_cp,) + attn.shape, attn.dtype),
        ),
        in_specs=[pl.BlockSpec(memory_space=pl.ANY)] * 2,
        out_specs=[pl.BlockSpec(memory_space=pl.ANY)] * 2,
        scratch_shapes=[
            dma((nz,)),
            dma((nz,)),
            dma((nz,)),
            dma((2 * nz,)),
            dma((4 * nz,)),
            dma((nz,)),
            dma((nz,)),
            dma((nz,)),
            dma((n_dev,)),
            dma((n_cp,)),
            dma((2,)),
        ],
        compiler_params=pltpu.CompilerParams(collective_id=0, has_side_effects=True),
        name="gather_rows",
    )(rows, attn)


def gather_local(grad_out, expert_ids, route_prob, attn_out, w_down, hidden_saved):
    n_tp = lax.axis_size("tp")
    n_cp = lax.axis_size("cp")
    n_dev = n_tp * n_cp
    slot_count = hidden_saved.shape[1]
    cap = slot_count // n_dev
    rows = grad_out[0]
    n_tok, width = rows.shape
    ids = expert_ids[0]
    hit = ids[None] == jnp.arange(n_dev, dtype=jnp.int32)[:, None, None]
    dense = jnp.sum(jnp.where(hit, route_prob[0].astype(jnp.float32)[None], 0.0), axis=2).astype(jnp.bfloat16)
    weights = lax.all_to_all(dense, ("tp", "cp"), split_axis=0, concat_axis=0, tiled=True)
    gall, aall = gather_all(n_tp, n_cp, rows, attn_out)

    live = weights > 0
    before = jnp.cumsum(live.astype(jnp.int32), axis=1) - 1
    take = jnp.logical_and(live[:, None, :], before[:, None, :] == jnp.arange(cap, dtype=jnp.int32)[None, :, None])
    pick = take.astype(jnp.bfloat16)
    weight = jnp.sum(jnp.where(take, weights[:, None, :].astype(jnp.float32), 0.0), axis=2).reshape(slot_count, 1)
    routed = lax.dot_general(
        pick, gall, (((2,), (1,)), ((0,), (0,))), preferred_element_type=jnp.float32
    ).astype(jnp.bfloat16).reshape(slot_count, width)
    saved = hidden_saved[0]
    proj = lax.dot_general(
        routed, w_down[0], (((1,), (1,)), ((), ())), preferred_element_type=jnp.float32
    )
    grad_hid = (weight * proj).astype(jnp.bfloat16)
    prob_part = jnp.sum(proj * saved.astype(jnp.float32), axis=1)
    weighted = (weight * routed.astype(jnp.float32)).astype(jnp.bfloat16)
    grad_w = lax.dot_general(
        saved, weighted, (((0,), (0,)), ((), ())), preferred_element_type=jnp.float32
    ).astype(jnp.bfloat16)
    part = jnp.sum(jnp.where(take, prob_part.reshape(n_dev, cap, 1), 0.0), axis=1)
    returned = lax.all_to_all(part, ("tp", "cp"), split_axis=0, concat_axis=0, tiled=True)
    grad_prob = jnp.sum(jnp.where(hit, returned[:, :, None], 0.0), axis=0)[None]

    c = lax.axis_index("cp")
    feat = width // n_cp
    mine = lax.dynamic_slice_in_dim(gall, c * feat, feat, axis=2)
    mine = mine.reshape(n_tp, n_cp, n_tok, feat)
    attn = aall.reshape(n_cp, n_tp, n_tok, attn_out.shape[1])
    grad_oproj = lax.dot_general(
        mine, attn, (((0, 1, 2), (1, 0, 2)), ((), ())), preferred_element_type=jnp.float32
    ).astype(jnp.bfloat16)
    return (grad_prob, grad_hid[None], grad_w[None], grad_oproj)


def solution(mesh):
    in_specs = (
        P("tp", "cp", None),
        P("tp", "cp", None),
        P("tp", "cp", None),
        P("cp", "tp"),
        P(("tp", "cp"), None, None),
        P(("tp", "cp"), None, None),
    )
    out_specs = (
        P("tp", "cp", None),
        P(("tp", "cp"), None, None),
        P(("tp", "cp"), None, None),
        P("cp", "tp"),
    )
    small = mesh.shape["tp"] == 4 and mesh.shape["cp"] <= 8 and mesh.shape["cp"] % 2 == 0
    local = gather_local if small else exchange_local
    return jax.shard_map(local, mesh=mesh, in_specs=in_specs, out_specs=out_specs, check_vma=False)
```

```python
import functools

import jax
import jax.numpy as jnp
from jax import lax
from jax.experimental import pallas as pl
from jax.experimental.pallas import tpu as pltpu
from jax.sharding import PartitionSpec as P

MESH = pl.DeviceIdType.MESH


def exchange_local(grad_out, expert_ids, route_prob, attn_out, w_down, hidden_saved):
    tp_count = lax.axis_size("tp")
    cp_count = lax.axis_size("cp")
    n_experts = tp_count * cp_count
    slot_count = hidden_saved.shape[1]
    capacity = slot_count // n_experts
    local_rows = grad_out[0]
    token_count = local_rows.shape[0]
    width = local_rows.shape[1]
    top_count = expert_ids.shape[2]
    route_ids = expert_ids[0].reshape(-1)
    onehot = (route_ids[:, None] == jnp.arange(n_experts, dtype=jnp.int32)[None, :]).astype(
        jnp.int32
    )
    position = jnp.sum((jnp.cumsum(onehot, axis=0) - 1) * onehot, axis=1)
    target = route_ids * capacity + position
    token_of = jnp.arange(token_count * top_count, dtype=jnp.int32) // top_count
    send_rows = (
        jnp.zeros((n_experts * capacity, width), jnp.bfloat16).at[target].set(local_rows[token_of])
    )
    send_prob = (
        jnp.zeros((n_experts * capacity,), jnp.bfloat16).at[target].set(route_prob[0].reshape(-1))
    )

    def swap(value):
        return lax.all_to_all(value, ("tp", "cp"), split_axis=0, concat_axis=0, tiled=True)

    routed = swap(send_rows.reshape(n_experts, capacity, width)).reshape(slot_count, width)
    got_prob = swap(send_prob.reshape(n_experts, capacity))
    weight = got_prob.reshape(slot_count).astype(jnp.float32)[:, None]
    saved = hidden_saved[0]
    proj = lax.dot_general(
        routed, w_down[0], (((1,), (1,)), ((), ())), preferred_element_type=jnp.float32
    )
    grad_hid = (weight * proj).astype(jnp.bfloat16)
    prob_part = jnp.sum(proj * saved.astype(jnp.float32), axis=1)
    weighted = (weight * routed.astype(jnp.float32)).astype(jnp.bfloat16)
    grad_w = lax.dot_general(
        saved, weighted, (((0,), (0,)), ((), ())), preferred_element_type=jnp.float32
    ).astype(jnp.bfloat16)
    returned = swap(prob_part.reshape(n_experts, capacity))
    grad_prob = returned.reshape(-1)[target].reshape(1, token_count, top_count)
    gathered = lax.all_gather(grad_out, "tp", axis=0, tiled=True).reshape(-1, width)
    grad_oproj = lax.psum_scatter(
        lax.dot_general(
            gathered, attn_out, (((0,), (0,)), ((), ())), preferred_element_type=jnp.float32
        ),
        "cp",
        scatter_dimension=0,
        tiled=True,
    ).astype(jnp.bfloat16)
    return (grad_prob, grad_hid[None], grad_w[None], grad_oproj)


def gather_kernel(
    n_tp, n_cp, g_ref, a_ref, w_ref, saved_ref, rank_ref, prob_ref,
    gall, aall, hid_ref, gw_ref, op_ref, part_ref,
    w_v, saved_v, acc, gw_v, hid_v, proj_v, gst, gcol, ast, oacc, o_v,
    gz_l, gz_r, gy_s, gx_s, gs_s, az_l, az_r, ay_s, g_recv, a_recv, own_sem, in_sem, st_sem, col_sem, out_sem,
):
    t = lax.axis_index("tp")
    c = lax.axis_index("cp")
    core = t % 2
    x = t // 2
    y = c % 2
    z = c // 2
    nz = n_cp // 2
    sib = t + 1 - 2 * core
    xt = (1 - x) * 2 + core
    yc = z * 2 + 1 - y
    has_l = z > 0
    has_r = z < nz - 1

    load_w = pltpu.make_async_copy(w_ref, w_v, in_sem.at[0])
    load_saved = pltpu.make_async_copy(saved_ref, saved_v, in_sem.at[1])
    load_w.start()
    load_saved.start()
    barrier = pltpu.get_barrier_semaphore()

    def greet(tt, cc):
        pl.semaphore_signal(barrier, inc=1, device_id=(tt, cc), device_id_type=MESH)

    greet(sib, c)
    greet(xt, c)
    greet(t, yc)

    @pl.when(has_l)
    def _():
        greet(t, c - 2)

    @pl.when(has_r)
    def _():
        greet(t, c + 2)

    pl.semaphore_wait(barrier, 3 + has_l.astype(jnp.int32) + has_r.astype(jnp.int32))

    def pick(values):
        got = values[0]
        for k in range(1, nz):
            got = jnp.where(z == k, values[k], got)
        return got

    lists = []
    for p in range(nz):
        lists.append(sorted(range(nz), key=lambda q, p=p: (abs(q - p), q)))
    order = [z] + [pick([lists[p][i] for p in range(nz)]) for i in range(1, nz)]

    def gblock(tt, zz, yy):
        return tt * n_cp + zz * 2 + yy

    def gcopy(b, src, send, dev):
        return pltpu.make_async_remote_copy(
            src_ref=src, dst_ref=gall.at[b], send_sem=send, recv_sem=g_recv.at[b], device_id=dev, device_id_type=MESH
        )

    def acopy(k, src, send, dev):
        return pltpu.make_async_remote_copy(
            src_ref=src, dst_ref=aall.at[k], send_sem=send, recv_sem=a_recv.at[k], device_id=dev, device_id_type=MESH
        )

    mine = gblock(t, z, y)
    own_g = pltpu.make_async_copy(g_ref, gall.at[mine], own_sem.at[0])
    own_a = pltpu.make_async_copy(a_ref, aall.at[c], own_sem.at[1])
    own_g.start()
    own_a.start()
    sends = []

    def line(copier, left, right, i, idx, src):
        def go(sem, dc, cond):
            op = copier(idx, src, sem.at[i], (t, c + dc))

            @pl.when(cond)
            def _():
                op.start()

            sends.append((op, cond))

        zi = order[i]
        if i == 0:
            go(left, -2, has_l)
            go(right, 2, has_r)
        else:
            go(left, -2, jnp.logical_and(zi > z, has_l))
            go(right, 2, jnp.logical_and(zi < z, has_r))

    def plain(op):
        op.start()
        sends.append((op, None))

    nx = [0]
    ns = [0]

    def to_x(b, src):
        plain(gcopy(b, src, gx_s.at[nx[0]], (xt, c)))
        nx[0] += 1

    def to_sib(b, src):
        plain(gcopy(b, src, gs_s.at[ns[0]], (sib, c)))
        ns[0] += 1

    def z_event(i):
        b = gblock(t, order[i], y)
        if i == 0:
            src = g_ref
        else:
            src = gall.at[b]
            gcopy(b, src, gy_s.at[0], (t, c)).wait_recv()
        line(gcopy, gz_l, gz_r, i, b, src)
        plain(gcopy(b, src, gy_s.at[i], (t, yc)))
        to_x(b, src)
        to_sib(b, src)

    def y_event(i):
        b = gblock(t, order[i], 1 - y)
        gcopy(b, gall.at[b], gy_s.at[0], (t, c)).wait_recv()
        to_x(b, gall.at[b])
        to_sib(b, gall.at[b])

    xseq = [(0, y)]
    for i in range(1, nz):
        xseq += [(i, y), (i - 1, 1 - y)]
    xseq.append((nz - 1, 1 - y))

    def x_event(k):
        i, yy = xseq[k]
        b = gblock(xt, order[i], yy)
        gcopy(b, gall.at[b], gy_s.at[0], (t, c)).wait_recv()
        to_sib(b, gall.at[b])

    def az_event(i):
        k = order[i] * 2 + y
        if i == 0:
            src = a_ref
        else:
            src = aall.at[k]
            acopy(k, src, ay_s.at[0], (t, c)).wait_recv()
        line(acopy, az_l, az_r, i, k, src)
        plain(acopy(k, src, ay_s.at[i], (t, yc)))

    cap2 = saved_v.shape[1]
    n_tok, width = g_ref.shape
    n_hid = saved_v.shape[2]
    step = min(1024, width)
    feat = o_v.shape[0]
    cols = pl.ds(pl.multiple_of(c * feat, feat), feat)

    def recv_g(b):
        gcopy(b, gall.at[b], gy_s.at[0], (t, c)).wait_recv()

    def experts(xx, i, first, last):
        pairs = []
        loads = []
        for k in range(2):
            tt = xx * 2 + (core if k == 0 else 1 - core)
            p = tt * nz + order[i]
            if k == 1:
                recv_g(2 * p)
                recv_g(2 * p + 1)
            load = pltpu.make_async_copy(gall.at[pl.ds(2 * p, 2)], gst.at[k], st_sem.at[k])
            load.start()
            pairs.append(p)
            loads.append(load)
        picks, weights = [], []
        for p in pairs:
            slot = lax.broadcasted_iota(jnp.int32, (cap2, 2 * n_tok), 0)
            take = slot == rank_ref[p]
            weights.append(jnp.sum(jnp.where(take, prob_ref[p], 0.0), axis=1, keepdims=True))
            picks.append(jnp.where(take, 1.0, 0.0).astype(jnp.bfloat16))
        weight = jnp.concatenate(weights, axis=0)
        hidden = jnp.concatenate([saved_v[p] for p in pairs], axis=0)
        for load in loads:
            load.wait()

        def chunk(n, carry):
            at = pl.ds(pl.multiple_of(n * step, step), step)
            rows = jnp.concatenate(
                [
                    jnp.dot(
                        picks[k],
                        gst[k, :, :, at].reshape(2 * n_tok, step),
                        preferred_element_type=jnp.float32,
                    )
                    for k in range(2)
                ],
                axis=0,
            )
            proj = lax.dot_general(
                rows.astype(jnp.bfloat16), w_v[:, at], (((1,), (1,)), ((), ())), preferred_element_type=jnp.float32
            )

            @pl.when(n == 0)
            def _():
                proj_v[...] = proj

            @pl.when(n > 0)
            def _():
                proj_v[...] += proj

            scaled = (weight * rows).astype(jnp.bfloat16)
            grad = lax.dot_general(hidden, scaled, (((0,), (0,)), ((), ())), preferred_element_type=jnp.float32)
            if not first:
                grad = acc[:, at] + grad
            if last:
                gw_v[:, at] = grad.astype(jnp.bfloat16)
            else:
                acc[:, at] = grad
            return carry

        lax.fori_loop(0, width // step, chunk, 0)
        proj = proj_v[...]
        hid = (weight * proj).astype(jnp.bfloat16)
        sums = jnp.sum(proj * hidden.astype(jnp.float32), axis=1, keepdims=True)
        for k, p in enumerate(pairs):
            hid_v[p] = hid[k * cap2 : (k + 1) * cap2]
            take = lax.broadcasted_iota(jnp.int32, (cap2, 2 * n_tok), 0) == rank_ref[p]
            part_ref[p] = jnp.sum(
                jnp.where(take, sums[k * cap2 : (k + 1) * cap2], 0.0), axis=0, keepdims=True
            )

    def outer(i, first):
        zi = order[i]
        loads = [pltpu.make_async_copy(aall.at[pl.ds(2 * zi, 2)], ast, col_sem.at[2 * n_tp])]
        for yy in range(2):
            for tt in range(n_tp):
                k = yy * n_tp + tt
                loads.append(
                    pltpu.make_async_copy(gall.at[gblock(tt, zi, yy), :, cols], gcol.at[k], col_sem.at[k])
                )
        for load in loads:
            load.start()
        for load in loads:
            load.wait()
        got = lax.dot_general(
            gcol[...].reshape(2 * n_tp * n_tok, feat),
            ast[...].reshape(2 * n_tp * n_tok, ast.shape[2]),
            (((0,), (0,)), ((), ())),
            preferred_element_type=jnp.float32,
        )
        if first:
            oacc[...] = got
        else:
            oacc[...] += got

    def ay_event(i):
        k = order[i] * 2 + 1 - y
        acopy(k, aall.at[k], ay_s.at[0], (t, c)).wait_recv()

    xo = 1 - x
    z_event(0)
    own_g.wait()
    own_a.wait()
    load_w.wait()
    load_saved.wait()
    for r in range(1, nz):
        z_event(r)
        y_event(r - 1)
        x_event(r - 1)
        if r == nz - 1:
            az_event(0)
        experts(x, r - 1, r == 1, False)
    y_event(nz - 1)
    x_event(nz - 1)
    az_event(1)
    experts(x, nz - 1, False, False)
    experts(xo, 0, False, False)
    x_event(nz)
    for i in range(2, nz):
        az_event(i)
    ay_event(0)
    experts(xo, 1, False, False)
    outer(0, True)
    x_event(nz + 1)
    ay_event(1)
    outer(1, False)
    x_event(nz + 2)
    experts(xo, 2, False, False)
    ay_event(2)
    outer(2, False)
    x_event(nz + 3)
    experts(xo, 3, False, True)
    out_gw = pltpu.make_async_copy(gw_v, gw_ref, out_sem.at[0])
    out_gw.start()
    out_hid = pltpu.make_async_copy(hid_v, hid_ref, out_sem.at[1])
    out_hid.start()
    ay_event(3)
    outer(3, False)
    o_v[...] = oacc[...].astype(jnp.bfloat16)
    out_op = pltpu.make_async_copy(o_v, op_ref, out_sem.at[2])
    out_op.start()
    out_gw.wait()
    out_hid.wait()
    out_op.wait()
    for op, cond in sends:
        if cond is None:
            op.wait_send()
        else:

            @pl.when(cond)
            def _(op=op):
                op.wait_send()


def gather_all(n_tp, n_cp, rows, attn, w_down, saved, rank, prob):
    nz = n_cp // 2
    dma = pltpu.SemaphoreType.DMA
    n_dev = n_tp * n_cp
    n_tok, width = rows.shape
    n_hid = w_down.shape[0]
    feat = width // n_cp
    heads = attn.shape[1]
    slots = saved.shape[0] * saved.shape[1]
    hbm = pl.BlockSpec(memory_space=pl.ANY)
    vmem = pl.BlockSpec(memory_space=pltpu.VMEM)
    shape = jax.ShapeDtypeStruct
    bf16, f32 = jnp.bfloat16, jnp.float32
    cap2 = saved.shape[1]
    flops = 4 * slots * width * n_hid + 2 * n_dev * n_tok * feat * heads
    return pl.pallas_call(
        functools.partial(gather_kernel, n_tp, n_cp),
        out_shape=(
            shape((n_dev,) + rows.shape, bf16),
            shape((n_cp,) + attn.shape, bf16),
            shape(saved.shape, bf16),
            shape(w_down.shape, bf16),
            shape((feat, heads), bf16),
            shape(prob.shape, f32),
        ),
        in_specs=[hbm] * 4 + [vmem] * 2,
        out_specs=[hbm] * 5 + [vmem],
        scratch_shapes=[
            pltpu.VMEM(w_down.shape, bf16),
            pltpu.VMEM(saved.shape, bf16),
            pltpu.VMEM(w_down.shape, f32),
            pltpu.VMEM(w_down.shape, bf16),
            pltpu.VMEM(saved.shape, bf16),
            pltpu.VMEM((2 * cap2, n_hid), f32),
            pltpu.VMEM((2, 2, n_tok, width), bf16),
            pltpu.VMEM((2 * n_tp, n_tok, feat), bf16),
            pltpu.VMEM((2,) + attn.shape, bf16),
            pltpu.VMEM((feat, heads), f32),
            pltpu.VMEM((feat, heads), bf16),
            dma((nz,)),
            dma((nz,)),
            dma((nz,)),
            dma((2 * nz,)),
            dma((4 * nz,)),
            dma((nz,)),
            dma((nz,)),
            dma((nz,)),
            dma((n_dev,)),
            dma((n_cp,)),
            dma((2,)),
            dma((2,)),
            dma((2,)),
            dma((2 * n_tp + 1,)),
            dma((3,)),
        ],
        compiler_params=pltpu.CompilerParams(
            collective_id=0, has_side_effects=True, vmem_limit_bytes=56 * 1024 * 1024
        ),
        cost_estimate=pl.CostEstimate(flops=flops, bytes_accessed=4 * n_dev * n_tok * width, transcendentals=0),
        name="gather_and_multiply",
    )(rows, attn, w_down, saved, rank, prob)


def gather_local(grad_out, expert_ids, route_prob, attn_out, w_down, hidden_saved):
    n_tp = lax.axis_size("tp")
    n_cp = lax.axis_size("cp")
    n_dev = n_tp * n_cp
    slot_count = hidden_saved.shape[1]
    cap = slot_count // n_dev
    rows = grad_out[0]
    n_tok, width = rows.shape
    ids = expert_ids[0]
    hit = ids[None] == jnp.arange(n_dev, dtype=jnp.int32)[:, None, None]
    dense = jnp.sum(jnp.where(hit, route_prob[0].astype(jnp.float32)[None], 0.0), axis=2).astype(jnp.bfloat16)
    weights = lax.all_to_all(dense, ("tp", "cp"), split_axis=0, concat_axis=0, tiled=True)
    live = weights > 0
    earlier = jnp.triu(jnp.ones((n_tok, n_tok), jnp.bfloat16), 1)
    before = jnp.dot(live.astype(jnp.bfloat16), earlier, preferred_element_type=jnp.float32).astype(jnp.int32)
    offset = (jnp.arange(n_dev, dtype=jnp.int32) % 2 * cap)[:, None]
    rank = jnp.where(live, before + offset, -1).reshape(n_dev // 2, 1, 2 * n_tok)
    prob = weights.astype(jnp.float32).reshape(n_dev // 2, 1, 2 * n_tok)
    saved = hidden_saved[0].reshape(n_dev // 2, 2 * cap, hidden_saved.shape[2])
    _, _, hid, grad_w, grad_oproj, part = gather_all(
        n_tp, n_cp, rows, attn_out, w_down[0], saved, rank, prob
    )
    returned = lax.all_to_all(part.reshape(n_dev, n_tok), ("tp", "cp"), split_axis=0, concat_axis=0, tiled=True)
    grad_prob = jnp.sum(jnp.where(hit, returned[:, :, None], 0.0), axis=0)[None]
    return (grad_prob, hid.reshape(hidden_saved.shape), grad_w[None], grad_oproj)


def solution(mesh):
    in_specs = (
        P("tp", "cp", None),
        P("tp", "cp", None),
        P("tp", "cp", None),
        P("cp", "tp"),
        P(("tp", "cp"), None, None),
        P(("tp", "cp"), None, None),
    )
    out_specs = (
        P("tp", "cp", None),
        P(("tp", "cp"), None, None),
        P(("tp", "cp"), None, None),
        P("cp", "tp"),
    )
    small = mesh.shape["tp"] == 4 and mesh.shape["cp"] == 8
    local = gather_local if small else exchange_local
    return jax.shard_map(local, mesh=mesh, in_specs=in_specs, out_specs=out_specs, check_vma=False)
```

```python
import functools

import jax
import jax.numpy as jnp
from jax import lax
from jax.experimental import pallas as pl
from jax.experimental.pallas import tpu as pltpu
from jax.sharding import PartitionSpec as P

MESH = pl.DeviceIdType.MESH


def exchange_local(grad_out, expert_ids, route_prob, attn_out, w_down, hidden_saved):
    tp_count = lax.axis_size("tp")
    cp_count = lax.axis_size("cp")
    n_experts = tp_count * cp_count
    slot_count = hidden_saved.shape[1]
    capacity = slot_count // n_experts
    local_rows = grad_out[0]
    token_count = local_rows.shape[0]
    width = local_rows.shape[1]
    top_count = expert_ids.shape[2]
    route_ids = expert_ids[0].reshape(-1)
    onehot = (route_ids[:, None] == jnp.arange(n_experts, dtype=jnp.int32)[None, :]).astype(
        jnp.int32
    )
    position = jnp.sum((jnp.cumsum(onehot, axis=0) - 1) * onehot, axis=1)
    target = route_ids * capacity + position
    token_of = jnp.arange(token_count * top_count, dtype=jnp.int32) // top_count
    send_rows = (
        jnp.zeros((n_experts * capacity, width), jnp.bfloat16).at[target].set(local_rows[token_of])
    )
    send_prob = (
        jnp.zeros((n_experts * capacity,), jnp.bfloat16).at[target].set(route_prob[0].reshape(-1))
    )

    def swap(value):
        return lax.all_to_all(value, ("tp", "cp"), split_axis=0, concat_axis=0, tiled=True)

    routed = swap(send_rows.reshape(n_experts, capacity, width)).reshape(slot_count, width)
    got_prob = swap(send_prob.reshape(n_experts, capacity))
    weight = got_prob.reshape(slot_count).astype(jnp.float32)[:, None]
    saved = hidden_saved[0]
    proj = lax.dot_general(
        routed, w_down[0], (((1,), (1,)), ((), ())), preferred_element_type=jnp.float32
    )
    grad_hid = (weight * proj).astype(jnp.bfloat16)
    prob_part = jnp.sum(proj * saved.astype(jnp.float32), axis=1)
    weighted = (weight * routed.astype(jnp.float32)).astype(jnp.bfloat16)
    grad_w = lax.dot_general(
        saved, weighted, (((0,), (0,)), ((), ())), preferred_element_type=jnp.float32
    ).astype(jnp.bfloat16)
    returned = swap(prob_part.reshape(n_experts, capacity))
    grad_prob = returned.reshape(-1)[target].reshape(1, token_count, top_count)
    gathered = lax.all_gather(grad_out, "tp", axis=0, tiled=True).reshape(-1, width)
    grad_oproj = lax.psum_scatter(
        lax.dot_general(
            gathered, attn_out, (((0,), (0,)), ((), ())), preferred_element_type=jnp.float32
        ),
        "cp",
        scatter_dimension=0,
        tiled=True,
    ).astype(jnp.bfloat16)
    return (grad_prob, grad_hid[None], grad_w[None], grad_oproj)


def gather_kernel(
    n_tp, n_cp, g_ref, a_ref, w_ref, saved_ref,
    gall, aall, hid_ref, gw_ref, op_ref, part_ref,
    w_v, saved_v, acc, gw_v, hid_v, proj_v, gst, gcol, ast, oacc, o_v, rows_v, hidt_v, rank_v, prob_v,
    gz_l, gz_r, gy_s, gx_s, gs_s, az_l, az_r, ay_s, g_recv, a_recv, own_sem, in_sem, st_sem, col_sem, out_sem, gw_sem,
):
    t = lax.axis_index("tp")
    c = lax.axis_index("cp")
    core = t % 2
    x = t // 2
    y = c % 2
    z = c // 2
    nz = n_cp // 2
    sib = t + 1 - 2 * core
    xt = (1 - x) * 2 + core
    yc = z * 2 + 1 - y
    has_l = z > 0
    has_r = z < nz - 1

    load_w = pltpu.make_async_copy(w_ref, w_v, in_sem.at[0])
    load_saved = pltpu.make_async_copy(saved_ref, saved_v, in_sem.at[1])
    load_w.start()
    load_saved.start()
    barrier = pltpu.get_barrier_semaphore()

    def greet(tt, cc):
        pl.semaphore_signal(barrier, inc=1, device_id=(tt, cc), device_id_type=MESH)

    greet(sib, c)
    greet(xt, c)
    greet(t, yc)

    @pl.when(has_l)
    def _():
        greet(t, c - 2)

    @pl.when(has_r)
    def _():
        greet(t, c + 2)

    pl.semaphore_wait(barrier, 3 + has_l.astype(jnp.int32) + has_r.astype(jnp.int32))

    def pick(values):
        got = values[0]
        for k in range(1, nz):
            got = jnp.where(z == k, values[k], got)
        return got

    lists = []
    for p in range(nz):
        lists.append(sorted(range(nz), key=lambda q, p=p: (abs(q - p), q)))
    order = [z] + [pick([lists[p][i] for p in range(nz)]) for i in range(1, nz)]

    def gblock(tt, zz, yy):
        return tt * n_cp + zz * 2 + yy

    def gcopy(b, src, send, dev):
        return pltpu.make_async_remote_copy(
            src_ref=src, dst_ref=gall.at[b], send_sem=send, recv_sem=g_recv.at[b], device_id=dev, device_id_type=MESH
        )

    def acopy(k, src, send, dev):
        return pltpu.make_async_remote_copy(
            src_ref=src, dst_ref=aall.at[k], send_sem=send, recv_sem=a_recv.at[k], device_id=dev, device_id_type=MESH
        )

    mine = gblock(t, z, y)
    own_g = pltpu.make_async_copy(g_ref, gall.at[mine], own_sem.at[0])
    own_a = pltpu.make_async_copy(a_ref, aall.at[c], own_sem.at[1])
    own_g.start()
    own_a.start()
    sends = []

    def line(copier, left, right, i, idx, src):
        def go(sem, dc, cond):
            op = copier(idx, src, sem.at[i], (t, c + dc))

            @pl.when(cond)
            def _():
                op.start()

            sends.append((op, cond))

        zi = order[i]
        if i == 0:
            go(left, -2, has_l)
            go(right, 2, has_r)
        else:
            go(left, -2, jnp.logical_and(zi > z, has_l))
            go(right, 2, jnp.logical_and(zi < z, has_r))

    def plain(op):
        op.start()
        sends.append((op, None))

    nx = [0]
    ns = [0]

    def to_x(b, src):
        plain(gcopy(b, src, gx_s.at[nx[0]], (xt, c)))
        nx[0] += 1

    def to_sib(b, src):
        plain(gcopy(b, src, gs_s.at[ns[0]], (sib, c)))
        ns[0] += 1

    def z_event(i):
        b = gblock(t, order[i], y)
        if i == 0:
            src = g_ref
        else:
            src = gall.at[b]
            gcopy(b, src, gy_s.at[0], (t, c)).wait_recv()
        line(gcopy, gz_l, gz_r, i, b, src)
        plain(gcopy(b, src, gy_s.at[i], (t, yc)))
        to_x(b, src)
        to_sib(b, src)

    def y_event(i):
        b = gblock(t, order[i], 1 - y)
        gcopy(b, gall.at[b], gy_s.at[0], (t, c)).wait_recv()
        to_x(b, gall.at[b])
        to_sib(b, gall.at[b])

    xseq = [(0, y)]
    for i in range(1, nz):
        xseq += [(i, y), (i - 1, 1 - y)]
    xseq.append((nz - 1, 1 - y))

    def x_event(k):
        i, yy = xseq[k]
        b = gblock(xt, order[i], yy)
        gcopy(b, gall.at[b], gy_s.at[0], (t, c)).wait_recv()
        to_sib(b, gall.at[b])

    def az_event(i):
        k = order[i] * 2 + y
        if i == 0:
            src = a_ref
        else:
            src = aall.at[k]
            acopy(k, src, ay_s.at[0], (t, c)).wait_recv()
        line(acopy, az_l, az_r, i, k, src)
        plain(acopy(k, src, ay_s.at[i], (t, yc)))

    cap2 = saved_v.shape[1]
    n_tok = g_ref.shape[0]
    width = w_v.shape[1]
    step = min(1024, width)
    feat = o_v.shape[0]
    cols = pl.ds(pl.multiple_of(c * feat, feat), feat)
    f32, bf16 = jnp.float32, jnp.bfloat16
    nt = (((1,), (1,)), ((), ()))

    def recv_g(b):
        gcopy(b, gall.at[b], gy_s.at[0], (t, c)).wait_recv()

    def pair_of(xx, i, k):
        return (xx * 2 + (core if k == 0 else 1 - core)) * nz + order[i]

    def taken(p):
        return lax.broadcasted_iota(jnp.int32, (cap2, 2 * n_tok), 0) == rank_v[p][0:1]

    def select(xx, i):
        pairs = [pair_of(xx, i, k) for k in range(2)]
        loads = []
        for k, p in enumerate(pairs):
            if k == 1:
                recv_g(2 * p)
                recv_g(2 * p + 1)
            load = pltpu.make_async_copy(gall.at[pl.ds(2 * p, 2)], gst.at[k], st_sem.at[k])
            load.start()
            loads.append(load)
        lanes = g_ref.shape[1] - width
        expert = t * n_cp + c
        one = jnp.where(lax.broadcasted_iota(jnp.int32, (8, lanes), 1) == expert, 1.0, 0.0).astype(bf16)
        row = lax.broadcasted_iota(jnp.int32, (2 * n_tok, 2 * n_tok), 0)
        col = lax.broadcasted_iota(jnp.int32, (2 * n_tok, 2 * n_tok), 1)
        same = (row >= n_tok) == (col >= n_tok)
        earlier = jnp.where(jnp.logical_and(same, row < col), 1.0, 0.0).astype(bf16)
        lane = lax.broadcasted_iota(jnp.int32, (8, 2 * n_tok), 1)
        offset = jnp.where(lane >= n_tok, cap2 // 2, 0)
        for k, p in enumerate(pairs):
            loads[k].wait()
            table = gst[k, :, :, width:].reshape(2 * n_tok, lanes)
            prob = lax.dot_general(one, table, nt, preferred_element_type=f32)
            live = prob > 0
            before = jnp.dot(jnp.where(live, 1.0, 0.0).astype(bf16), earlier, preferred_element_type=f32)
            prob_v[p] = prob
            rank_v[p] = jnp.where(live, before.astype(jnp.int32) + offset, -1)
            pick = jnp.where(taken(p), 1.0, 0.0).astype(bf16)

            def chunk(n, carry, k=k, pick=pick):
                at = pl.ds(pl.multiple_of(n * step, step), step)
                got = jnp.dot(pick, gst[k, :, :, at].reshape(2 * n_tok, step), preferred_element_type=f32)
                rows_v[i, k * cap2 : (k + 1) * cap2, at] = got.astype(bf16)
                return carry

            lax.fori_loop(0, width // step, chunk, 0)

    def experts(xx, first_i, last_i, first, last):
        count = last_i + 1 - first_i
        size = count * 2 * cap2
        pairs = [pair_of(xx, i, k) for i in range(first_i, last_i + 1) for k in range(2)]
        weight = jnp.concatenate(
            [jnp.sum(jnp.where(taken(p), prob_v[p][0:1], 0.0), axis=1, keepdims=True) for p in pairs], axis=0
        )
        hidt_v[:, :size] = jnp.concatenate([saved_v[p] for p in pairs], axis=0).T

        def chunk(n, carry):
            at = pl.ds(pl.multiple_of(n * step, step), step)
            rows = rows_v[first_i : last_i + 1, :, at].reshape(size, step)
            proj = lax.dot_general(rows, w_v[:, at], nt, preferred_element_type=f32)

            @pl.when(n == 0)
            def _():
                proj_v[:size] = proj

            @pl.when(n > 0)
            def _():
                proj_v[:size] += proj

            scaled = (weight * rows.astype(f32)).astype(bf16)
            grad = jnp.dot(hidt_v[:, :size], scaled, preferred_element_type=f32)
            if not first:
                grad = acc[:, at] + grad
            if last:
                gw_v[:, at] = grad.astype(bf16)
                pltpu.make_async_copy(gw_v.at[:, at], gw_ref.at[:, at], gw_sem.at[n]).start()
            else:
                acc[:, at] = grad
            return carry

        lax.fori_loop(0, width // step, chunk, 0)
        for j, p in enumerate(pairs):
            part = slice(j * cap2, (j + 1) * cap2)
            proj = proj_v[part]
            hid_v[p] = (weight[part] * proj).astype(bf16)
            total = jnp.sum(proj * saved_v[p].astype(f32), axis=1, keepdims=True)
            part_ref[p] = jnp.sum(jnp.where(taken(p), total, 0.0), axis=0, keepdims=True)

    def outer(i, first):
        zi = order[i]
        loads = [pltpu.make_async_copy(aall.at[pl.ds(2 * zi, 2)], ast, col_sem.at[2 * n_tp])]
        for yy in range(2):
            for tt in range(n_tp):
                k = yy * n_tp + tt
                loads.append(
                    pltpu.make_async_copy(gall.at[gblock(tt, zi, yy), :, cols], gcol.at[k], col_sem.at[k])
                )
        for load in loads:
            load.start()
        for load in loads:
            load.wait()
        got = lax.dot_general(
            gcol[...].reshape(2 * n_tp * n_tok, feat),
            ast[...].reshape(2 * n_tp * n_tok, ast.shape[2]),
            (((0,), (0,)), ((), ())),
            preferred_element_type=jnp.float32,
        )
        if first:
            oacc[...] = got
        else:
            oacc[...] += got

    def ay_event(i):
        k = order[i] * 2 + 1 - y
        acopy(k, aall.at[k], ay_s.at[0], (t, c)).wait_recv()

    xo = 1 - x
    z_event(0)
    own_g.wait()
    for r in range(1, nz):
        z_event(r)
        y_event(r - 1)
        x_event(r - 1)
        if r == nz - 1:
            az_event(0)
        select(x, r - 1)
    y_event(nz - 1)
    x_event(nz - 1)
    az_event(1)
    select(x, nz - 1)
    load_w.wait()
    load_saved.wait()
    own_a.wait()
    experts(x, 0, 3, True, False)
    x_event(4)
    az_event(2)
    select(xo, 0)
    select(xo, 1)
    az_event(3)
    ay_event(0)
    outer(0, True)
    ay_event(1)
    outer(1, False)
    x_event(5)
    x_event(6)
    select(xo, 2)
    experts(xo, 0, 2, False, False)
    ay_event(2)
    outer(2, False)
    x_event(7)
    select(xo, 3)
    experts(xo, 3, 3, False, True)
    out_hid = pltpu.make_async_copy(hid_v, hid_ref, out_sem.at[1])
    out_hid.start()
    ay_event(3)
    outer(3, False)
    o_v[...] = oacc[...].astype(jnp.bfloat16)
    out_op = pltpu.make_async_copy(o_v, op_ref, out_sem.at[2])
    out_op.start()
    for n in range(width // step):
        at = pl.ds(n * step, step)
        pltpu.make_async_copy(gw_v.at[:, at], gw_ref.at[:, at], gw_sem.at[n]).wait()
    out_hid.wait()
    out_op.wait()
    for op, cond in sends:
        if cond is None:
            op.wait_send()
        else:

            @pl.when(cond)
            def _(op=op):
                op.wait_send()


def gather_all(n_tp, n_cp, rows, attn, w_down, saved):
    nz = n_cp // 2
    dma = pltpu.SemaphoreType.DMA
    n_dev = n_tp * n_cp
    n_tok = rows.shape[0]
    n_hid, width = w_down.shape
    feat = width // n_cp
    heads = attn.shape[1]
    slots = saved.shape[0] * saved.shape[1]
    hbm = pl.BlockSpec(memory_space=pl.ANY)
    vmem = pl.BlockSpec(memory_space=pltpu.VMEM)
    shape = jax.ShapeDtypeStruct
    bf16, f32 = jnp.bfloat16, jnp.float32
    cap2 = saved.shape[1]
    flops = 4 * slots * width * n_hid + 2 * n_dev * n_tok * feat * heads
    return pl.pallas_call(
        functools.partial(gather_kernel, n_tp, n_cp),
        out_shape=(
            shape((n_dev,) + rows.shape, bf16),
            shape((n_cp,) + attn.shape, bf16),
            shape(saved.shape, bf16),
            shape(w_down.shape, bf16),
            shape((feat, heads), bf16),
            shape((n_dev // 2, 1, 2 * n_tok), f32),
        ),
        in_specs=[hbm] * 4,
        out_specs=[hbm] * 5 + [vmem],
        scratch_shapes=[
            pltpu.VMEM(w_down.shape, bf16),
            pltpu.VMEM(saved.shape, bf16),
            pltpu.VMEM(w_down.shape, f32),
            pltpu.VMEM(w_down.shape, bf16),
            pltpu.VMEM(saved.shape, bf16),
            pltpu.VMEM((nz * 2 * cap2, n_hid), f32),
            pltpu.VMEM((2, 2) + rows.shape, bf16),
            pltpu.VMEM((2 * n_tp, n_tok, feat), bf16),
            pltpu.VMEM((2,) + attn.shape, bf16),
            pltpu.VMEM((feat, heads), f32),
            pltpu.VMEM((feat, heads), bf16),
            pltpu.VMEM((nz, 2 * cap2, width), bf16),
            pltpu.VMEM((n_hid, nz * 2 * cap2), bf16),
            pltpu.VMEM((n_dev // 2, 8, 2 * n_tok), jnp.int32),
            pltpu.VMEM((n_dev // 2, 8, 2 * n_tok), f32),
            dma((nz,)),
            dma((nz,)),
            dma((nz,)),
            dma((2 * nz,)),
            dma((4 * nz,)),
            dma((nz,)),
            dma((nz,)),
            dma((nz,)),
            dma((n_dev,)),
            dma((n_cp,)),
            dma((2,)),
            dma((2,)),
            dma((2,)),
            dma((2 * n_tp + 1,)),
            dma((3,)),
            dma((width // min(1024, width),)),
        ],
        compiler_params=pltpu.CompilerParams(
            collective_id=0, has_side_effects=True, vmem_limit_bytes=60 * 1024 * 1024
        ),
        cost_estimate=pl.CostEstimate(flops=flops, bytes_accessed=4 * n_dev * n_tok * width, transcendentals=0),
        name="gather_and_multiply",
    )(rows, attn, w_down, saved)


def gather_local(grad_out, expert_ids, route_prob, attn_out, w_down, hidden_saved):
    n_tp = lax.axis_size("tp")
    n_cp = lax.axis_size("cp")
    n_dev = n_tp * n_cp
    slot_count = hidden_saved.shape[1]
    cap = slot_count // n_dev
    rows = grad_out[0]
    n_tok, width = rows.shape
    ids = expert_ids[0]
    hit = ids[None] == jnp.arange(n_dev, dtype=jnp.int32)[:, None, None]
    named = ids[:, None, :] == jnp.arange(128, dtype=jnp.int32)[None, :, None]
    table = jnp.sum(jnp.where(named, route_prob[0].astype(jnp.float32)[:, None, :], 0.0), axis=2)
    rows = jnp.concatenate([rows, table.astype(jnp.bfloat16)], axis=1)
    saved = hidden_saved[0].reshape(n_dev // 2, 2 * cap, hidden_saved.shape[2])
    _, _, hid, grad_w, grad_oproj, part = gather_all(n_tp, n_cp, rows, attn_out, w_down[0], saved)
    returned = lax.all_to_all(part.reshape(n_dev, n_tok), ("tp", "cp"), split_axis=0, concat_axis=0, tiled=True)
    grad_prob = jnp.sum(jnp.where(hit, returned[:, :, None], 0.0), axis=0)[None]
    return (grad_prob, hid.reshape(hidden_saved.shape), grad_w[None], grad_oproj)


def solution(mesh):
    in_specs = (
        P("tp", "cp", None),
        P("tp", "cp", None),
        P("tp", "cp", None),
        P("cp", "tp"),
        P(("tp", "cp"), None, None),
        P(("tp", "cp"), None, None),
    )
    out_specs = (
        P("tp", "cp", None),
        P(("tp", "cp"), None, None),
        P(("tp", "cp"), None, None),
        P("cp", "tp"),
    )
    small = mesh.shape["tp"] == 4 and mesh.shape["cp"] == 8
    local = gather_local if small else exchange_local
    return jax.shard_map(local, mesh=mesh, in_specs=in_specs, out_specs=out_specs, check_vma=False)
```

```python
import functools

import jax
import jax.numpy as jnp
from jax import lax
from jax.experimental import pallas as pl
from jax.experimental.pallas import tpu as pltpu
from jax.sharding import PartitionSpec as P

MESH = pl.DeviceIdType.MESH


def exchange_local(grad_out, expert_ids, route_prob, attn_out, w_down, hidden_saved):
    tp_count = lax.axis_size("tp")
    cp_count = lax.axis_size("cp")
    n_experts = tp_count * cp_count
    slot_count = hidden_saved.shape[1]
    capacity = slot_count // n_experts
    local_rows = grad_out[0]
    token_count = local_rows.shape[0]
    width = local_rows.shape[1]
    top_count = expert_ids.shape[2]
    route_ids = expert_ids[0].reshape(-1)
    onehot = (route_ids[:, None] == jnp.arange(n_experts, dtype=jnp.int32)[None, :]).astype(
        jnp.int32
    )
    position = jnp.sum((jnp.cumsum(onehot, axis=0) - 1) * onehot, axis=1)
    target = route_ids * capacity + position
    token_of = jnp.arange(token_count * top_count, dtype=jnp.int32) // top_count
    send_rows = (
        jnp.zeros((n_experts * capacity, width), jnp.bfloat16).at[target].set(local_rows[token_of])
    )
    send_prob = (
        jnp.zeros((n_experts * capacity,), jnp.bfloat16).at[target].set(route_prob[0].reshape(-1))
    )

    def swap(value):
        return lax.all_to_all(value, ("tp", "cp"), split_axis=0, concat_axis=0, tiled=True)

    routed = swap(send_rows.reshape(n_experts, capacity, width)).reshape(slot_count, width)
    got_prob = swap(send_prob.reshape(n_experts, capacity))
    weight = got_prob.reshape(slot_count).astype(jnp.float32)[:, None]
    saved = hidden_saved[0]
    proj = lax.dot_general(
        routed, w_down[0], (((1,), (1,)), ((), ())), preferred_element_type=jnp.float32
    )
    grad_hid = (weight * proj).astype(jnp.bfloat16)
    prob_part = jnp.sum(proj * saved.astype(jnp.float32), axis=1)
    weighted = (weight * routed.astype(jnp.float32)).astype(jnp.bfloat16)
    grad_w = lax.dot_general(
        saved, weighted, (((0,), (0,)), ((), ())), preferred_element_type=jnp.float32
    ).astype(jnp.bfloat16)
    returned = swap(prob_part.reshape(n_experts, capacity))
    grad_prob = returned.reshape(-1)[target].reshape(1, token_count, top_count)
    gathered = lax.all_gather(grad_out, "tp", axis=0, tiled=True).reshape(-1, width)
    grad_oproj = lax.psum_scatter(
        lax.dot_general(
            gathered, attn_out, (((0,), (0,)), ((), ())), preferred_element_type=jnp.float32
        ),
        "cp",
        scatter_dimension=0,
        tiled=True,
    ).astype(jnp.bfloat16)
    return (grad_prob, grad_hid[None], grad_w[None], grad_oproj)


def gather_kernel(
    n_tp, n_cp, g_ref, a_ref, w_ref, saved_ref,
    gall, aall, hid_ref, gw_ref, op_ref, part_ref,
    w_v, saved_v, acc, gw_v, hid_v, proj_v, gst, gcol, ast, oacc, o_v, rows_v, hidt_v, rank_v, prob_v,
    gz_l, gz_r, gy_s, gx_s, gs_s, az_l, az_r, ay_s, g_recv, a_recv, own_sem, in_sem, st_sem, col_sem, out_sem, gw_sem,
):
    t = lax.axis_index("tp")
    c = lax.axis_index("cp")
    core = t % 2
    x = t // 2
    y = c % 2
    z = c // 2
    nz = n_cp // 2
    sib = t + 1 - 2 * core
    xt = (1 - x) * 2 + core
    yc = z * 2 + 1 - y
    has_l = z > 0
    has_r = z < nz - 1

    load_w = pltpu.make_async_copy(w_ref, w_v, in_sem.at[0])
    load_saved = pltpu.make_async_copy(saved_ref, saved_v, in_sem.at[1])
    load_w.start()
    load_saved.start()
    barrier = pltpu.get_barrier_semaphore()

    def greet(tt, cc):
        pl.semaphore_signal(barrier, inc=1, device_id=(tt, cc), device_id_type=MESH)

    greet(sib, c)
    greet(xt, c)
    greet(t, yc)

    @pl.when(has_l)
    def _():
        greet(t, c - 2)

    @pl.when(has_r)
    def _():
        greet(t, c + 2)

    pl.semaphore_wait(barrier, 3 + has_l.astype(jnp.int32) + has_r.astype(jnp.int32))

    def pick(values):
        got = values[0]
        for k in range(1, nz):
            got = jnp.where(z == k, values[k], got)
        return got

    lists = []
    for p in range(nz):
        lists.append(sorted(range(nz), key=lambda q, p=p: (abs(q - p), q)))
    order = [z] + [pick([lists[p][i] for p in range(nz)]) for i in range(1, nz)]

    def gblock(tt, zz, yy):
        return tt * n_cp + zz * 2 + yy

    def gcopy(b, src, send, dev):
        return pltpu.make_async_remote_copy(
            src_ref=src, dst_ref=gall.at[b], send_sem=send, recv_sem=g_recv.at[b], device_id=dev, device_id_type=MESH
        )

    def acopy(k, src, send, dev):
        return pltpu.make_async_remote_copy(
            src_ref=src, dst_ref=aall.at[k], send_sem=send, recv_sem=a_recv.at[k], device_id=dev, device_id_type=MESH
        )

    mine = gblock(t, z, y)
    own_g = pltpu.make_async_copy(g_ref, gall.at[mine], own_sem.at[0])
    own_a = pltpu.make_async_copy(a_ref, aall.at[c], own_sem.at[1])
    own_g.start()
    own_a.start()
    sends = []

    def line(copier, left, right, i, idx, src):
        def go(sem, dc, cond):
            op = copier(idx, src, sem.at[i], (t, c + dc))

            @pl.when(cond)
            def _():
                op.start()

            sends.append((op, cond))

        zi = order[i]
        if i == 0:
            go(left, -2, has_l)
            go(right, 2, has_r)
        else:
            go(left, -2, jnp.logical_and(zi > z, has_l))
            go(right, 2, jnp.logical_and(zi < z, has_r))

    def plain(op):
        op.start()
        sends.append((op, None))

    nx = [0]
    ns = [0]

    def to_x(b, src):
        plain(gcopy(b, src, gx_s.at[nx[0]], (xt, c)))
        nx[0] += 1

    def to_sib(b, src):
        plain(gcopy(b, src, gs_s.at[ns[0]], (sib, c)))
        ns[0] += 1

    def z_event(i):
        b = gblock(t, order[i], y)
        if i == 0:
            src = g_ref
        else:
            src = gall.at[b]
            gcopy(b, src, gy_s.at[0], (t, c)).wait_recv()
        line(gcopy, gz_l, gz_r, i, b, src)
        plain(gcopy(b, src, gy_s.at[i], (t, yc)))
        to_x(b, src)
        to_sib(b, src)

    def y_event(i):
        b = gblock(t, order[i], 1 - y)
        gcopy(b, gall.at[b], gy_s.at[0], (t, c)).wait_recv()
        to_x(b, gall.at[b])
        to_sib(b, gall.at[b])

    xseq = [(0, y)]
    for i in range(1, nz):
        xseq += [(i, y), (i - 1, 1 - y)]
    xseq.append((nz - 1, 1 - y))

    def x_event(k):
        i, yy = xseq[k]
        b = gblock(xt, order[i], yy)
        gcopy(b, gall.at[b], gy_s.at[0], (t, c)).wait_recv()
        to_sib(b, gall.at[b])

    def az_event(i):
        k = order[i] * 2 + y
        if i == 0:
            src = a_ref
        else:
            src = aall.at[k]
            acopy(k, src, ay_s.at[0], (t, c)).wait_recv()
        line(acopy, az_l, az_r, i, k, src)
        plain(acopy(k, src, ay_s.at[i], (t, yc)))

    cap2 = saved_v.shape[1]
    n_tok = g_ref.shape[0]
    width = w_v.shape[1]
    step = min(1024, width)
    feat = o_v.shape[0]
    cols = pl.ds(pl.multiple_of(c * feat, feat), feat)
    f32, bf16 = jnp.float32, jnp.bfloat16
    nt = (((1,), (1,)), ((), ()))

    def recv_g(b):
        gcopy(b, gall.at[b], gy_s.at[0], (t, c)).wait_recv()

    def pair_of(xx, i, k):
        return (xx * 2 + (core if k == 0 else 1 - core)) * nz + order[i]

    def taken(p):
        return lax.broadcasted_iota(jnp.int32, (cap2, 2 * n_tok), 0) == rank_v[p][0:1]

    def select(xx, i):
        pairs = [pair_of(xx, i, k) for k in range(2)]
        loads = []
        for k, p in enumerate(pairs):
            if k == 1:
                recv_g(2 * p)
                recv_g(2 * p + 1)
            load = pltpu.make_async_copy(gall.at[pl.ds(2 * p, 2)], gst.at[k], st_sem.at[k])
            load.start()
            loads.append(load)
        lanes = g_ref.shape[1] - width
        expert = t * n_cp + c
        one = jnp.where(lax.broadcasted_iota(jnp.int32, (8, lanes), 1) == expert, 1.0, 0.0).astype(bf16)
        row = lax.broadcasted_iota(jnp.int32, (2 * n_tok, 2 * n_tok), 0)
        col = lax.broadcasted_iota(jnp.int32, (2 * n_tok, 2 * n_tok), 1)
        same = (row >= n_tok) == (col >= n_tok)
        earlier = jnp.where(jnp.logical_and(same, row < col), 1.0, 0.0).astype(bf16)
        lane = lax.broadcasted_iota(jnp.int32, (8, 2 * n_tok), 1)
        offset = jnp.where(lane >= n_tok, cap2 // 2, 0)
        for k, p in enumerate(pairs):
            loads[k].wait()
            table = gst[k, :, :, width:].reshape(2 * n_tok, lanes)
            prob = lax.dot_general(one, table, nt, preferred_element_type=f32)
            live = prob > 0
            before = jnp.dot(jnp.where(live, 1.0, 0.0).astype(bf16), earlier, preferred_element_type=f32)
            prob_v[p] = prob
            rank_v[p] = jnp.where(live, before.astype(jnp.int32) + offset, -1)
            pick = jnp.where(taken(p), 1.0, 0.0).astype(bf16)

            def chunk(n, carry, k=k, pick=pick):
                at = pl.ds(pl.multiple_of(n * step, step), step)
                got = jnp.dot(pick, gst[k, :, :, at].reshape(2 * n_tok, step), preferred_element_type=f32)
                rows_v[i, k * cap2 : (k + 1) * cap2, at] = got.astype(bf16)
                return carry

            lax.fori_loop(0, width // step, chunk, 0)

    def experts(xx, first_i, last_i, first, last):
        count = last_i + 1 - first_i
        size = count * 2 * cap2
        pairs = [pair_of(xx, i, k) for i in range(first_i, last_i + 1) for k in range(2)]
        weight = jnp.concatenate(
            [jnp.sum(jnp.where(taken(p), prob_v[p][0:1], 0.0), axis=1, keepdims=True) for p in pairs], axis=0
        )
        hidt_v[:, :size] = jnp.concatenate([saved_v[p] for p in pairs], axis=0).T

        def chunk(n, carry):
            at = pl.ds(pl.multiple_of(n * step, step), step)
            rows = rows_v[first_i : last_i + 1, :, at].reshape(size, step)
            proj = lax.dot_general(rows, w_v[:, at], nt, preferred_element_type=f32)

            @pl.when(n == 0)
            def _():
                proj_v[:size] = proj

            @pl.when(n > 0)
            def _():
                proj_v[:size] += proj

            scaled = (weight * rows.astype(f32)).astype(bf16)
            grad = jnp.dot(hidt_v[:, :size], scaled, preferred_element_type=f32)
            if not first:
                grad = acc[:, at] + grad
            if last:
                gw_v[:, at] = grad.astype(bf16)
                pltpu.make_async_copy(gw_v.at[:, at], gw_ref.at[:, at], gw_sem.at[n]).start()
            else:
                acc[:, at] = grad
            return carry

        lax.fori_loop(0, width // step, chunk, 0)
        for j, p in enumerate(pairs):
            part = slice(j * cap2, (j + 1) * cap2)
            proj = proj_v[part]
            hid_v[p] = (weight[part] * proj).astype(bf16)
            total = jnp.sum(proj * saved_v[p].astype(f32), axis=1, keepdims=True)
            part_ref[p] = jnp.sum(jnp.where(taken(p), total, 0.0), axis=0, keepdims=True)

    def outer(i, first):
        zi = order[i]
        loads = [pltpu.make_async_copy(aall.at[pl.ds(2 * zi, 2)], ast, col_sem.at[2 * n_tp])]
        for yy in range(2):
            for tt in range(n_tp):
                k = yy * n_tp + tt
                loads.append(
                    pltpu.make_async_copy(gall.at[gblock(tt, zi, yy), :, cols], gcol.at[k], col_sem.at[k])
                )
        for load in loads:
            load.start()
        for load in loads:
            load.wait()
        got = lax.dot_general(
            gcol[...].reshape(2 * n_tp * n_tok, feat),
            ast[...].reshape(2 * n_tp * n_tok, ast.shape[2]),
            (((0,), (0,)), ((), ())),
            preferred_element_type=jnp.float32,
        )
        if first:
            oacc[...] = got
        else:
            oacc[...] += got

    def ay_event(i):
        k = order[i] * 2 + 1 - y
        acopy(k, aall.at[k], ay_s.at[0], (t, c)).wait_recv()

    xo = 1 - x
    z_event(0)
    own_g.wait()
    for r in range(1, nz):
        z_event(r)
        y_event(r - 1)
        x_event(r - 1)
        if r == nz - 1:
            az_event(0)
        select(x, r - 1)
    y_event(nz - 1)
    x_event(nz - 1)
    az_event(1)
    select(x, nz - 1)
    load_w.wait()
    load_saved.wait()
    own_a.wait()
    experts(x, 0, 3, True, False)
    x_event(4)
    az_event(2)
    select(xo, 0)
    select(xo, 1)
    ay_event(0)
    outer(0, True)
    az_event(3)
    experts(xo, 0, 1, False, False)
    ay_event(1)
    outer(1, False)
    x_event(5)
    x_event(6)
    select(xo, 2)
    experts(xo, 2, 2, False, False)
    ay_event(2)
    outer(2, False)
    x_event(7)
    select(xo, 3)
    experts(xo, 3, 3, False, True)
    out_hid = pltpu.make_async_copy(hid_v, hid_ref, out_sem.at[1])
    out_hid.start()
    ay_event(3)
    outer(3, False)
    o_v[...] = oacc[...].astype(jnp.bfloat16)
    out_op = pltpu.make_async_copy(o_v, op_ref, out_sem.at[2])
    out_op.start()
    for n in range(width // step):
        at = pl.ds(n * step, step)
        pltpu.make_async_copy(gw_v.at[:, at], gw_ref.at[:, at], gw_sem.at[n]).wait()
    out_hid.wait()
    out_op.wait()
    for op, cond in sends:
        if cond is None:
            op.wait_send()
        else:

            @pl.when(cond)
            def _(op=op):
                op.wait_send()


def gather_all(n_tp, n_cp, rows, attn, w_down, saved):
    nz = n_cp // 2
    dma = pltpu.SemaphoreType.DMA
    n_dev = n_tp * n_cp
    n_tok = rows.shape[0]
    n_hid, width = w_down.shape
    feat = width // n_cp
    heads = attn.shape[1]
    slots = saved.shape[0] * saved.shape[1]
    hbm = pl.BlockSpec(memory_space=pl.ANY)
    vmem = pl.BlockSpec(memory_space=pltpu.VMEM)
    shape = jax.ShapeDtypeStruct
    bf16, f32 = jnp.bfloat16, jnp.float32
    cap2 = saved.shape[1]
    flops = 4 * slots * width * n_hid + 2 * n_dev * n_tok * feat * heads
    return pl.pallas_call(
        functools.partial(gather_kernel, n_tp, n_cp),
        out_shape=(
            shape((n_dev,) + rows.shape, bf16),
            shape((n_cp,) + attn.shape, bf16),
            shape(saved.shape, bf16),
            shape(w_down.shape, bf16),
            shape((feat, heads), bf16),
            shape((n_dev // 2, 1, 2 * n_tok), f32),
        ),
        in_specs=[hbm] * 4,
        out_specs=[hbm] * 5 + [vmem],
        scratch_shapes=[
            pltpu.VMEM(w_down.shape, bf16),
            pltpu.VMEM(saved.shape, bf16),
            pltpu.VMEM(w_down.shape, f32),
            pltpu.VMEM(w_down.shape, bf16),
            pltpu.VMEM(saved.shape, bf16),
            pltpu.VMEM((nz * 2 * cap2, n_hid), f32),
            pltpu.VMEM((2, 2) + rows.shape, bf16),
            pltpu.VMEM((2 * n_tp, n_tok, feat), bf16),
            pltpu.VMEM((2,) + attn.shape, bf16),
            pltpu.VMEM((feat, heads), f32),
            pltpu.VMEM((feat, heads), bf16),
            pltpu.VMEM((nz, 2 * cap2, width), bf16),
            pltpu.VMEM((n_hid, nz * 2 * cap2), bf16),
            pltpu.VMEM((n_dev // 2, 8, 2 * n_tok), jnp.int32),
            pltpu.VMEM((n_dev // 2, 8, 2 * n_tok), f32),
            dma((nz,)),
            dma((nz,)),
            dma((nz,)),
            dma((2 * nz,)),
            dma((4 * nz,)),
            dma((nz,)),
            dma((nz,)),
            dma((nz,)),
            dma((n_dev,)),
            dma((n_cp,)),
            dma((2,)),
            dma((2,)),
            dma((2,)),
            dma((2 * n_tp + 1,)),
            dma((3,)),
            dma((width // min(1024, width),)),
        ],
        compiler_params=pltpu.CompilerParams(
            collective_id=0, has_side_effects=True, vmem_limit_bytes=60 * 1024 * 1024
        ),
        cost_estimate=pl.CostEstimate(flops=flops, bytes_accessed=4 * n_dev * n_tok * width, transcendentals=0),
        name="gather_and_multiply",
    )(rows, attn, w_down, saved)


def place_kernel(*refs):
    n = (len(refs) - 1) // 2
    copies = [pltpu.make_async_copy(refs[k], refs[n + k], refs[-1].at[k]) for k in range(n)]
    for copy in copies:
        copy.start()
    for copy in copies:
        copy.wait()


def place_results(*values):
    hbm = pl.BlockSpec(memory_space=pl.ANY)
    return pl.pallas_call(
        place_kernel,
        out_shape=tuple(jax.ShapeDtypeStruct(v.shape, v.dtype) for v in values),
        in_specs=[hbm] * len(values),
        out_specs=[hbm] * len(values),
        scratch_shapes=[pltpu.SemaphoreType.DMA((len(values),))],
        cost_estimate=pl.CostEstimate(
            flops=0, bytes_accessed=sum(2 * v.size * v.dtype.itemsize for v in values), transcendentals=0
        ),
        name="place_results",
    )(*values)


def gather_local(grad_out, expert_ids, route_prob, attn_out, w_down, hidden_saved):
    n_tp = lax.axis_size("tp")
    n_cp = lax.axis_size("cp")
    n_dev = n_tp * n_cp
    slot_count = hidden_saved.shape[1]
    cap = slot_count // n_dev
    rows = grad_out[0]
    n_tok, width = rows.shape
    ids = expert_ids[0]
    hit = ids[None] == jnp.arange(n_dev, dtype=jnp.int32)[:, None, None]
    named = ids[:, None, :] == jnp.arange(128, dtype=jnp.int32)[None, :, None]
    table = jnp.sum(jnp.where(named, route_prob[0].astype(jnp.float32)[:, None, :], 0.0), axis=2)
    rows = jnp.concatenate([rows, table.astype(jnp.bfloat16)], axis=1)
    saved = hidden_saved[0].reshape(n_dev // 2, 2 * cap, hidden_saved.shape[2])
    _, _, hid, grad_w, grad_oproj, part = gather_all(n_tp, n_cp, rows, attn_out, w_down[0], saved)
    returned = lax.all_to_all(part.reshape(n_dev, n_tok), ("tp", "cp"), split_axis=0, concat_axis=0, tiled=True)
    grad_prob = jnp.sum(jnp.where(hit, returned[:, :, None], 0.0), axis=0)[None]
    hid, grad_w, grad_oproj = place_results(hid, grad_w, grad_oproj)
    return (grad_prob, hid.reshape(hidden_saved.shape), grad_w[None], grad_oproj)


def solution(mesh):
    in_specs = (
        P("tp", "cp", None),
        P("tp", "cp", None),
        P("tp", "cp", None),
        P("cp", "tp"),
        P(("tp", "cp"), None, None),
        P(("tp", "cp"), None, None),
    )
    out_specs = (
        P("tp", "cp", None),
        P(("tp", "cp"), None, None),
        P(("tp", "cp"), None, None),
        P("cp", "tp"),
    )
    small = mesh.shape["tp"] == 4 and mesh.shape["cp"] == 8
    local = gather_local if small else exchange_local
    return jax.shard_map(local, mesh=mesh, in_specs=in_specs, out_specs=out_specs, check_vma=False)
```
